32 devices in a mesh: replica: 2 (over y), expert: 8 (over z, core), tensor: 2 (over x).
Axes of the slice: x: 2, y: 2, z: 4, core: 2. Of those that a mesh axis runs over, the one named last changes fastest.
Arguments:
- tokens: bfloat16 [672, 4096], P(('replica', 'expert'), 'tensor'), parts along dimension 0, may hold values from -6 to 6
- route_ids: int32 [672, 8], P(('replica', 'expert')), parts along dimension 0, may hold values from 0 to 15, all different within a row; in each aligned block of 42 rows (0 to 41, 42 to 83, ...) at most 42 rows name the same one
- route_scores: float32 [672, 8], P(('replica', 'expert')), parts along dimension 0, may hold values from 0.05 to 1
- w_gate: bfloat16 [16, 4096, 1536], P('expert', 'tensor'), may hold values from -0.09375 to 0.09375
- w_up: bfloat16 [16, 4096, 1536], P('expert', 'tensor'), may hold values from -0.09375 to 0.09375
- w_down: bfloat16 [16, 1536, 4096], P('expert', None, 'tensor'), may hold values from -0.15625 to 0.15625
Outputs:
- mixed: bfloat16 [672, 4096], P(('replica', 'expert'), 'tensor'), parts along dimension 0
The draws below stay inside these ranges and needn't reach their ends.
There are 2 independent parts, one for each index of `replica`. The reference program is written for one: setup_inputs(seed, part) draws one part's arguments, and reference() takes and returns one part's arrays. A program takes and returns all parts, laid end to end along the dimension named above; an argument that names none is the same for every part. Nothing has to cross between parts.
Inputs may be any that keep to these rules, and one draw needn't show every extreme that they name: `route_ids`: each row names 8 different experts. Within the rows of one index of the expert axis no expert is named by more than 42 rows, a bound that some block reaches of them.
All inputs are finite; a program needn't handle non-finite values.
Results may differ from the reference program's by a relative error of at most 0.0049.
Values may be sent and summed in bfloat16 or wider, within the bound.
No kernel may reach another device: no remote copies, remote signals or barrier semaphores. Data moves between devices by JAX's collectives and lax.ppermute only.
A program may use at most 128 MiB of HBM per device.

```python
import math
import jax
import jax.numpy as jnp
import numpy as np
from jax import lax

D = 4096
FF = 1536
TOP = 8
ROWS_DEV = 42
TOKENS = 336
EXPERTS = 16
CAP = 42
N_EXPERT = 8


def level_of(own_key, dims, shards, low, top_value):
    level = 1.0
    for axis_at, parts in shards:
        steps = jax.random.uniform(jax.random.fold_in(jax.random.fold_in(own_key, 6), axis_at), (parts,), jnp.float32, low / len(shards), top_value / len(shards))
        level = level * jnp.repeat(jnp.exp(steps), dims[axis_at] // parts).reshape((-1,) + (1,) * (len(dims) - 1 - axis_at))
    return level


def routed_block(rng, own, number, rows, count, top, bound, lean):
    ranking = jax.random.permutation(rng, count)
    heavy_load, ordinary = load_shares(count, rows * top, bound, lean, True), load_shares(count, rows * top, bound, lean, False)
    places = jnp.arange(count)

    def named(tallies, turn):
        used = int((tallies > 0).sum())
        fixed = max(1, used // 4)
        moved = fixed + (places - fixed + turn * (used - fixed)) % max(1, count - fixed)
        return jnp.zeros((count,), jnp.int32).at[ranking[jnp.where(places < fixed, places, moved)]].set(jnp.asarray(tallies, jnp.int32))

    tallies = jnp.where(number % 4 == 0, named(heavy_load, number // 4), named(ordinary, number - number // 4 - 1))
    mixed = jax.random.permutation(jax.random.fold_in(own, 3), count)
    source_of, receiver = mixed[0:count // 2 * 2:2], mixed[1:count // 2 * 2:2]
    slack = jnp.minimum(tallies[source_of] - 1, bound - tallies[receiver]) // 2
    slack = jnp.where((source_of == ranking[0]) | (receiver == ranking[0]) | (tallies[receiver] == 0), 0, jnp.maximum(slack, 0))
    moved = jax.random.randint(jax.random.fold_in(own, 4), (count // 2,), 0, 1 << 20) % (slack + 1)
    tallies = tallies.at[source_of].add(-moved).at[receiver].add(moved)
    labels = jnp.searchsorted(jnp.cumsum(tallies), jnp.arange(rows * top), side="right").astype(jnp.int32)
    grid = labels.reshape(top, rows).T
    grid = grid[jax.random.permutation(jax.random.fold_in(own, 1), rows)]
    turn = jax.random.randint(jax.random.fold_in(own, 2), (rows, 1), 0, top)
    return jnp.take_along_axis(grid, (jnp.arange(top)[None, :] + turn) % top, axis=1)


def load_shares(number_of, total, most, skew, full):
    portions = [(1 << 20) // math.isqrt(rank ** skew) + 1 for rank in range(1, number_of + 1)]
    largest = most if full else min(most, max(-(-total // number_of), total * portions[0] // sum(portions)))
    least = 1 if total - largest >= number_of - 1 else 0
    holding, spare = [largest] + [least] * (number_of - 1), total - largest - least * (number_of - 1)
    while spare > 0:
        candidates = [i for i in range(1, number_of) if holding[i] < largest] or [i for i in range(1, number_of) if holding[i] < most]
        mass, budget = sum([portions[i] for i in candidates]), spare
        for i in candidates:
            extra = min(most - holding[i], max(1, budget * portions[i] // mass), spare)
            holding[i] = holding[i] + extra
            spare = spare - extra
    return np.array(holding)


def centred(rng, shape, spread, most, split=(), kind=jnp.bfloat16):
    factor_of = level_of(rng, shape, split, -0.22, 0.18) if split else 1.0
    values = jax.random.normal(rng, shape, jnp.float32) * spread * factor_of
    return jnp.minimum(jnp.maximum(values, -most), most).astype(kind)


def setup_inputs(seed: int = 0, part: int = 0) -> dict:
    keys = jax.random.split(jax.random.key(seed), 7)
    part_splits = jax.random.split(jax.random.fold_in(keys[6], part), 7)
    tokens = centred(part_splits[0], (TOKENS, D), 1.0, 6.0, ((0, 8), (1, 2)))
    route_ids_keys = jax.random.split(jax.random.fold_in(part_splits[1], 1), TOKENS // ROWS_DEV)
    route_ids_turns = jax.random.permutation(jax.random.fold_in(part_splits[1], 3), TOKENS // ROWS_DEV)
    route_ids = jax.vmap(lambda own, number: routed_block(jax.random.fold_in(part_splits[1], 2), own, number, ROWS_DEV, EXPERTS, TOP, CAP, 2))(route_ids_keys, route_ids_turns).reshape((TOKENS, TOP))
    route_scores = jnp.clip(jnp.exp(math.log(1.0) - 2.9957323 * jax.random.uniform(part_splits[2], (TOKENS, TOP), jnp.float32) ** level_of(part_splits[2], (TOKENS, TOP), ((0, 8),), -0.2, 0.2)), 0.05, 1.0)
    w_gate = centred(keys[3], (EXPERTS, D, FF), D ** -0.5, 0.09375, ((0, 8), (1, 2)))
    w_up = centred(keys[4], (EXPERTS, D, FF), D ** -0.5, 0.09375, ((0, 8), (1, 2)))
    w_down = centred(keys[5], (EXPERTS, FF, D), FF ** -0.5, 0.15625, ((0, 8), (2, 2)))
    return {"tokens": tokens, "route_ids": route_ids, "route_scores": route_scores, "w_gate": w_gate, "w_up": w_up, "w_down": w_down}


def reference(tokens, route_ids, route_scores, w_gate, w_up, w_down):
    weights = route_scores / jnp.sum(route_scores, axis=1, keepdims=True)
    row_limit = N_EXPERT * CAP
    slot_range = jnp.arange(row_limit, dtype=jnp.int32)

    def add_expert(expert, total):
        hit_mask = route_ids == expert
        chosen = jnp.any(hit_mask, axis=1)
        row_share = jnp.sum(jnp.where(hit_mask, weights, jnp.zeros_like(weights)), axis=1)
        row_index = jnp.nonzero(chosen, size=row_limit, fill_value=0)[0].astype(jnp.int32)
        live_mask = slot_range < jnp.sum(chosen.astype(jnp.int32))
        chosen_rows = tokens[row_index]
        gate_part = jnp.dot(chosen_rows, w_gate[expert], preferred_element_type=jnp.float32)
        up_part = jnp.dot(chosen_rows, w_up[expert], preferred_element_type=jnp.float32)
        hidden = (jax.nn.silu(gate_part) * up_part).astype(jnp.bfloat16)
        produced = jnp.dot(hidden, w_down[expert], preferred_element_type=jnp.float32)
        factor = jnp.where(live_mask, row_share[row_index], jnp.zeros_like(row_share[row_index]))
        return total.at[row_index].add(produced * factor[:, None])

    total = lax.fori_loop(0, EXPERTS, add_expert, jnp.zeros((tokens.shape[0], tokens.shape[1]), jnp.float32))
    return total.astype(jnp.bfloat16)
```

```python
import functools

import jax
import jax.numpy as jnp
from jax import lax
from jax.experimental import pallas as pl
from jax.experimental.pallas import tpu as pltpu
from jax.sharding import PartitionSpec as P

CORES = 2
VMEM_LIMIT = 40 * 1024 * 1024


def slot_targets(chosen_ids, total_experts, capacity):
    expert_range = jnp.arange(total_experts, dtype=jnp.int32)
    hit_count = jnp.sum(
        (chosen_ids[:, :, None] == expert_range[None, None, :]).astype(jnp.int32), axis=1
    )
    before = jnp.cumsum(hit_count, axis=0) - hit_count
    return chosen_ids * capacity + jnp.take_along_axis(before, chosen_ids, axis=1)


def general_shards(tokens, route_ids, route_scores, w_gate, w_up, w_down):
    groups = lax.axis_size("expert")
    local_experts = w_gate.shape[0]
    count_rows = route_ids.shape[0]
    top_count = route_ids.shape[1]
    total_experts = groups * local_experts
    capacity = min(count_rows, 2 * count_rows * top_count // total_experts)
    slot_count = total_experts * capacity
    weights = route_scores / jnp.sum(route_scores, axis=1, keepdims=True)
    targets = slot_targets(route_ids, total_experts, capacity)
    row_width = tokens.shape[1]
    row_owner = jnp.broadcast_to(
        jnp.arange(count_rows, dtype=jnp.int32)[:, None], targets.shape
    ).reshape(-1)
    flat_index = targets.reshape(-1)
    source_row = jnp.zeros((slot_count,), jnp.int32).at[flat_index].set(row_owner)
    filled = jnp.zeros((slot_count,), jnp.bfloat16).at[flat_index].set(1.0)
    outgoing = (jnp.take(tokens, source_row, axis=0) * filled[:, None]).reshape(
        groups, local_experts, capacity, row_width
    )
    received = lax.all_to_all(outgoing, "expert", split_axis=0, concat_axis=0, tiled=True)
    gate_part = jnp.einsum("necd,edh->nech", received, w_gate, preferred_element_type=jnp.float32)
    up_part = jnp.einsum("necd,edh->nech", received, w_up, preferred_element_type=jnp.float32)
    gate_full, up_full = lax.psum((gate_part, up_part), "tensor")
    hidden = (jax.nn.silu(gate_full) * up_full).astype(jnp.bfloat16)
    produced = jnp.einsum("nech,ehd->necd", hidden, w_down, preferred_element_type=jnp.float32)
    returned = lax.all_to_all(produced, "expert", split_axis=0, concat_axis=0, tiled=True)
    returned = returned.reshape(slot_count, returned.shape[3])
    picked = jnp.take(returned, targets, axis=0)
    combined = jnp.sum(weights[:, :, None] * picked, axis=1)
    return combined.astype(jnp.bfloat16)


def gate_up_kernel(side_ref, rows_ref, gate_ref, up_ref, out_ref):
    rows = rows_ref[...]
    out_ref[0, 0] = jnp.dot(rows, gate_ref[0], preferred_element_type=jnp.float32).astype(out_ref.dtype)
    out_ref[0, 1] = jnp.dot(rows, up_ref[0], preferred_element_type=jnp.float32).astype(out_ref.dtype)


def gate_up(side, rows, w_gate, w_up, dtype):
    count = rows.shape[0]
    experts, width, units = w_gate.shape
    half = units // 2
    tile = 256
    steps = half // tile
    weight_spec = pl.BlockSpec((1, width, tile), lambda e, j, side: (e, 0, side[0] * steps + j))
    return pl.pallas_call(
        gate_up_kernel,
        out_shape=jax.ShapeDtypeStruct((experts, 2, count, half), dtype),
        grid_spec=pltpu.PrefetchScalarGridSpec(
            num_scalar_prefetch=1,
            grid=(experts, steps),
            in_specs=[
                pl.BlockSpec((count, width), lambda e, j, side: (0, 0)),
                weight_spec,
                weight_spec,
            ],
            out_specs=pl.BlockSpec((1, 2, count, tile), lambda e, j, side: (e, 0, 0, j)),
        ),
        compiler_params=pltpu.CompilerParams(vmem_limit_bytes=VMEM_LIMIT),
        cost_estimate=pl.CostEstimate(
            flops=4 * count * width * half * experts,
            bytes_accessed=4 * experts * width * half,
            transcendentals=0,
        ),
        name="gate_up",
    )(side, rows, w_gate, w_up)


def down_kernel(first, side_ref, hidden_ref, weight_ref, *refs):
    out_ref = refs[-1]
    product = jnp.dot(hidden_ref[0], weight_ref[0], preferred_element_type=jnp.float32)
    at_start = (pl.program_id(0) == 0) & (pl.program_id(1) == 0)

    @pl.when(at_start)
    def _():
        out_ref[...] = product if first else refs[0][...] + product

    @pl.when(jnp.logical_not(at_start))
    def _():
        out_ref[...] += product


def down(side, hidden, w_down, so_far):
    experts, count, half = hidden.shape
    width = w_down.shape[2]
    depth = 384
    steps = half // depth
    extra = [] if so_far is None else [so_far]
    whole = pl.BlockSpec((count, width), lambda e, j, side: (0, 0))
    return pl.pallas_call(
        functools.partial(down_kernel, so_far is None),
        out_shape=jax.ShapeDtypeStruct((count, width), jnp.float32),
        grid_spec=pltpu.PrefetchScalarGridSpec(
            num_scalar_prefetch=1,
            grid=(experts, steps),
            in_specs=[
                pl.BlockSpec((1, count, depth), lambda e, j, side: (e, 0, j)),
                pl.BlockSpec((1, depth, width), lambda e, j, side: (e, side[0] * steps + j, 0)),
            ]
            + [whole for _ in extra],
            out_specs=whole,
        ),
        compiler_params=pltpu.CompilerParams(vmem_limit_bytes=VMEM_LIMIT),
        cost_estimate=pl.CostEstimate(
            flops=2 * count * width * half * experts,
            bytes_accessed=2 * experts * width * half,
            transcendentals=0,
        ),
        name="down",
    )(side, hidden, w_down, *extra)


def pair_shards(tokens, route_ids, route_scores, w_gate, w_up, w_down):
    groups = lax.axis_size("expert")
    local_experts = w_gate.shape[0]
    count, width = tokens.shape
    w_gate, w_up, w_down = (
        pltpu.with_memory_space_constraint(w, pltpu.HBM) for w in (w_gate, w_up, w_down)
    )
    total_experts = groups * local_experts
    chips = groups // CORES
    here = lax.axis_index("expert")
    mine = lax.axis_index("tensor").reshape(1)
    other = 1 - mine

    def swap_tensor(value):
        return lax.ppermute(value, "tensor", [(0, 1), (1, 0)])

    def swap_expert(value, mask):
        return lax.ppermute(value, "expert", [(i, i ^ mask) for i in range(groups)])

    weights = route_scores / jnp.sum(route_scores, axis=1, keepdims=True)
    hit = route_ids[:, :, None] == jnp.arange(total_experts, dtype=jnp.int32)[None, None, :]
    share = jnp.sum(jnp.where(hit, weights[:, :, None], 0.0), axis=1)
    share_high = share.astype(jnp.bfloat16)
    share_low = (share - share_high.astype(jnp.float32)).astype(jnp.bfloat16)
    pad = -(2 * total_experts) % 128
    sent = jnp.concatenate(
        [tokens, share_high, share_low, jnp.zeros((count, pad), jnp.bfloat16)], axis=1
    )

    arrived = []
    for step in range(chips):
        same = swap_expert(sent, CORES * step) if step else sent
        arrived.append((same, swap_expert(same, 1)))

    def share_of(rows):
        high = lax.dynamic_slice(rows, (0, width + here * local_experts), (rows.shape[0], local_experts))
        low = lax.dynamic_slice(
            rows, (0, width + total_experts + here * local_experts), (rows.shape[0], local_experts)
        )
        return (high.astype(jnp.float32) + low.astype(jnp.float32)).T[:, :, None]

    order = [0] + [s for s in range(2, chips)] + [1] if chips > 1 else [0]
    total = None
    parts = {}
    for step in order:
        rows = jnp.concatenate(arrived[step], axis=0)
        theirs = gate_up(other, rows, w_gate, w_up, jnp.bfloat16)
        received = swap_tensor(theirs)
        kept = gate_up(mine, rows, w_gate, w_up, jnp.float32)
        full = kept + received.astype(jnp.float32)
        hidden = (jax.nn.silu(full[:, 0]) * full[:, 1] * share_of(rows)).astype(jnp.bfloat16)
        hidden_other = swap_tensor(hidden)
        product = down(mine, hidden, w_down, None)
        product = down(other, hidden_other, w_down, product)
        from_core = swap_expert(product[count:].astype(jnp.bfloat16), 1)
        summed = product[:count] + from_core.astype(jnp.float32)
        if step:
            summed = swap_expert(summed.astype(jnp.bfloat16), CORES * step).astype(jnp.float32)
        parts[step] = summed
    total = parts[0]
    for step in range(1, chips):
        total = total + parts[step]
    return total.astype(jnp.bfloat16)


def solution(mesh):
    groups = mesh.shape["expert"]
    paired = mesh.shape["tensor"] == 2 and groups % CORES == 0 and groups & (groups - 1) == 0
    placed = (
        P(("replica", "expert"), "tensor"),
        P(("replica", "expert"), None),
        P(("replica", "expert"), None),
        P("expert", "tensor", None),
        P("expert", "tensor", None),
        P("expert", None, "tensor"),
    )
    return jax.shard_map(
        pair_shards if paired else general_shards,
        mesh=mesh,
        in_specs=placed,
        out_specs=P(("replica", "expert"), "tensor"),
        check_vma=False,
    )
```

```python
import functools

import jax
import jax.numpy as jnp
from jax import lax
from jax.experimental import pallas as pl
from jax.experimental.pallas import tpu as pltpu
from jax.sharding import PartitionSpec as P

CORES = 2
EXTRA = 128
SMALL = 6 * 1024 * 1024
VMEM_SPEC = pl.BlockSpec(memory_space=pltpu.VMEM)
SMEM_SPEC = pl.BlockSpec(memory_space=pltpu.SMEM)
ANY_SPEC = pl.BlockSpec(memory_space=pl.ANY)


def in_hbm(value):
    return pltpu.with_memory_space_constraint(value, pltpu.HBM)


def in_vmem(value):
    return pltpu.with_memory_space_constraint(value, pltpu.VMEM)


def slot_targets(chosen_ids, total_experts, capacity):
    expert_range = jnp.arange(total_experts, dtype=jnp.int32)
    hit_count = jnp.sum(
        (chosen_ids[:, :, None] == expert_range[None, None, :]).astype(jnp.int32), axis=1
    )
    before = jnp.cumsum(hit_count, axis=0) - hit_count
    return chosen_ids * capacity + jnp.take_along_axis(before, chosen_ids, axis=1)


def general_shards(tokens, route_ids, route_scores, w_gate, w_up, w_down):
    groups = lax.axis_size("expert")
    local_experts = w_gate.shape[0]
    count_rows = route_ids.shape[0]
    top_count = route_ids.shape[1]
    total_experts = groups * local_experts
    capacity = min(count_rows, 2 * count_rows * top_count // total_experts)
    slot_count = total_experts * capacity
    weights = route_scores / jnp.sum(route_scores, axis=1, keepdims=True)
    targets = slot_targets(route_ids, total_experts, capacity)
    row_width = tokens.shape[1]
    row_owner = jnp.broadcast_to(
        jnp.arange(count_rows, dtype=jnp.int32)[:, None], targets.shape
    ).reshape(-1)
    flat_index = targets.reshape(-1)
    source_row = jnp.zeros((slot_count,), jnp.int32).at[flat_index].set(row_owner)
    filled = jnp.zeros((slot_count,), jnp.bfloat16).at[flat_index].set(1.0)
    outgoing = (jnp.take(tokens, source_row, axis=0) * filled[:, None]).reshape(
        groups, local_experts, capacity, row_width
    )
    received = lax.all_to_all(outgoing, "expert", split_axis=0, concat_axis=0, tiled=True)
    gate_part = jnp.einsum("necd,edh->nech", received, w_gate, preferred_element_type=jnp.float32)
    up_part = jnp.einsum("necd,edh->nech", received, w_up, preferred_element_type=jnp.float32)
    gate_full, up_full = lax.psum((gate_part, up_part), "tensor")
    hidden = (jax.nn.silu(gate_full) * up_full).astype(jnp.bfloat16)
    produced = jnp.einsum("nech,ehd->necd", hidden, w_down, preferred_element_type=jnp.float32)
    returned = lax.all_to_all(produced, "expert", split_axis=0, concat_axis=0, tiled=True)
    returned = returned.reshape(slot_count, returned.shape[3])
    picked = jnp.take(returned, targets, axis=0)
    combined = jnp.sum(weights[:, :, None] * picked, axis=1)
    return combined.astype(jnp.bfloat16)


def prepare_kernel(tokens_ref, ids_ref, scores_ref, out_ref):
    count, width = tokens_ref.shape
    top = ids_ref.shape[1]
    scores = scores_ref[...]
    weights = scores / jnp.sum(scores, axis=1, keepdims=True)
    lane = lax.broadcasted_iota(jnp.int32, (count, EXTRA), 1)
    ids = ids_ref[...]
    share = jnp.zeros((count, EXTRA), jnp.float32)
    for k in range(top):
        chosen = ids[:, k : k + 1]
        match = (lane == chosen) | (lane == chosen + EXTRA // 2)
        share = share + jnp.where(match, weights[:, k : k + 1], 0.0)
    high = share.astype(jnp.bfloat16).astype(jnp.float32)
    out_ref[:, :width] = tokens_ref[...]
    out_ref[:, width:] = jnp.where(lane < EXTRA // 2, high, share - high).astype(jnp.bfloat16)


def prepare(tokens, ids, scores):
    count, width = tokens.shape
    return pl.pallas_call(
        prepare_kernel,
        in_specs=[VMEM_SPEC] * 3,
        out_specs=VMEM_SPEC,
        out_shape=jax.ShapeDtypeStruct((count, width + EXTRA), jnp.bfloat16),
        compiler_params=pltpu.CompilerParams(vmem_limit_bytes=SMALL),
        name="prepare",
    )(tokens, ids, scores)


def project(rows_ref, held, out_ref, expert, which, start, size):
    width, half = held.shape[1:]
    place = (2 * expert + which) * half + start
    out_ref[:, place : place + size] = jnp.dot(
        rows_ref[:, :width], held[expert, :, start : start + size], preferred_element_type=jnp.float32
    ).astype(out_ref.dtype)


def gate_up_load_kernel(compute, side_ref, rows_ref, gate_ref, up_ref, *refs):
    gate_held, up_held, sem = refs[-3:]
    experts, _, half = gate_held.shape
    tile = half // 2
    base = side_ref[0] * half
    work = []
    for e in range(experts):
        for which, source, held in ((0, gate_ref, gate_held), (1, up_ref, up_held)):
            for start in range(0, half, tile):
                copy = pltpu.make_async_copy(
                    source.at[e, :, pl.ds(pl.multiple_of(base + start, 128), tile)],
                    held.at[e, :, pl.ds(start, tile)],
                    sem.at[len(work)],
                )
                copy.start()
                work.append((copy, held, e, which, start))
    for copy, held, e, which, start in work:
        copy.wait()
        if compute:
            project(rows_ref, held, refs[-4], e, which, start, tile)


def gate_up_load(side, rows, w_gate, w_up, after, dtype=None):
    count = rows.shape[0]
    experts, width, units = w_gate.shape
    half = units // 2
    compute = dtype is not None
    held = pltpu.VMEM((experts, width, half), w_gate.dtype)
    out = [jax.ShapeDtypeStruct((count, 2 * experts * half), dtype)] if compute else []
    return pl.pallas_call(
        functools.partial(gate_up_load_kernel, compute),
        in_specs=[SMEM_SPEC, VMEM_SPEC if compute else ANY_SPEC] + [ANY_SPEC] * (2 + len(after)),
        out_specs=[VMEM_SPEC] * (2 + len(out)),
        out_shape=out + [held, held],
        scratch_shapes=[pltpu.SemaphoreType.DMA((4 * experts,))],
        compiler_params=pltpu.CompilerParams(vmem_limit_bytes=SMALL),
        cost_estimate=pl.CostEstimate(
            flops=4 * count * width * half * experts,
            bytes_accessed=4 * experts * width * half,
            transcendentals=0,
        ),
        name="gate_up_load",
    )(side, rows, in_hbm(w_gate), in_hbm(w_up), *after)


def gate_up_kernel(rows_ref, gate_held, up_held, *refs):
    out_ref = refs[-1]
    experts, _, half = gate_held.shape
    tile = half // 3
    for e in range(experts):
        for which, held in ((0, gate_held), (1, up_held)):
            for start in range(0, half, tile):
                project(rows_ref, held, out_ref, e, which, start, tile)


def gate_up(rows, gate_held, up_held, dtype, after):
    count = rows.shape[0]
    experts, width, half = gate_held.shape
    return pl.pallas_call(
        gate_up_kernel,
        in_specs=[VMEM_SPEC] * 3 + [ANY_SPEC] * len(after),
        out_specs=VMEM_SPEC,
        out_shape=jax.ShapeDtypeStruct((count, 2 * experts * half), dtype),
        compiler_params=pltpu.CompilerParams(vmem_limit_bytes=SMALL),
        cost_estimate=pl.CostEstimate(
            flops=4 * max(count, 256) * width * half * experts,
            bytes_accessed=0,
            transcendentals=0,
        ),
        name="gate_up",
    )(rows, in_vmem(gate_held), in_vmem(up_held), *after)


def hidden_kernel(experts, here_ref, rows_ref, kept_ref, received_ref, *refs):
    out_ref = refs[-1]
    count = rows_ref.shape[0]
    half = kept_ref.shape[1] // (2 * experts)
    width = rows_ref.shape[1] - EXTRA
    share = rows_ref[:, width:].astype(jnp.float32)
    lane = lax.broadcasted_iota(jnp.int32, (count, EXTRA), 1)

    def full(index):
        columns = slice(index * half, (index + 1) * half)
        return kept_ref[:, columns] + received_ref[:, columns].astype(jnp.float32)

    for e in range(experts):
        expert = here_ref[0] * experts + e
        match = (lane == expert) | (lane == expert + EXTRA // 2)
        own = jnp.sum(jnp.where(match, share, 0.0), axis=1, keepdims=True)
        gate, up = full(2 * e), full(2 * e + 1)
        value = gate / (1.0 + jnp.exp(-gate)) * up * own
        out_ref[:, e * half : (e + 1) * half] = value.astype(out_ref.dtype)


def hidden_of(here, rows, kept, received, experts, after):
    count = kept.shape[0]
    half = kept.shape[1] // (2 * experts)
    return pl.pallas_call(
        functools.partial(hidden_kernel, experts),
        in_specs=[SMEM_SPEC] + [VMEM_SPEC] * 3 + [ANY_SPEC] * len(after),
        out_specs=VMEM_SPEC,
        out_shape=jax.ShapeDtypeStruct((count, experts * half), jnp.bfloat16),
        compiler_params=pltpu.CompilerParams(vmem_limit_bytes=SMALL),
        cost_estimate=pl.CostEstimate(
            flops=8 * count * half * experts,
            bytes_accessed=0,
            transcendentals=count * half * experts,
        ),
        name="hidden",
    )(here, rows, kept, received, *after)


def down_kernel(load, more, n_after, *refs):
    refs = list(refs)
    side_ref = refs.pop(0) if load else None
    hidden_ref, weight_ref = refs.pop(0), refs.pop(0)
    so_far = refs.pop(0) if more else None
    refs = refs[n_after:]
    out_ref = refs.pop(0)
    held, sem = refs if load else (weight_ref, None)
    experts, half, width = held.shape
    tile = width // 4
    copies = []
    if load:
        base = pl.multiple_of(side_ref[0] * half, 256)
        for index in range(4):
            for e in range(experts):
                columns = pl.ds(index * tile, tile)
                copy = pltpu.make_async_copy(
                    weight_ref.at[e, pl.ds(base, half), columns],
                    held.at[e, :, columns],
                    sem.at[len(copies)],
                )
                copy.start()
                copies.append(copy)
    for index in range(4):
        columns = slice(index * tile, (index + 1) * tile)
        value = so_far[:, columns] if more else None
        for e in range(experts):
            if load:
                copies[index * experts + e].wait()
            product = jnp.dot(
                hidden_ref[:, e * half : (e + 1) * half],
                held[e, :, columns],
                preferred_element_type=jnp.float32,
            )
            value = product if value is None else value + product
        out_ref[:, columns] = value.astype(out_ref.dtype)


def down(hidden, so_far, dtype, after, held=None, side=None, weight=None):
    count = hidden.shape[0]
    load = weight is not None
    more = so_far is not None
    experts, depth, width = (weight if load else held).shape
    half = depth // 2 if load else depth
    out = jax.ShapeDtypeStruct((count, width), dtype)
    operands = [side, hidden, in_hbm(weight)] if load else [hidden, in_vmem(held)]
    specs = [SMEM_SPEC, VMEM_SPEC, ANY_SPEC] if load else [VMEM_SPEC] * 2
    if more:
        operands.append(so_far)
        specs.append(VMEM_SPEC)
    operands += after
    specs += [ANY_SPEC] * len(after)
    return pl.pallas_call(
        functools.partial(down_kernel, load, more, len(after)),
        in_specs=specs,
        out_specs=[VMEM_SPEC] * 2 if load else VMEM_SPEC,
        out_shape=[out, pltpu.VMEM((experts, half, width), weight.dtype)] if load else out,
        scratch_shapes=[pltpu.SemaphoreType.DMA((4 * experts,))] if load else [],
        compiler_params=pltpu.CompilerParams(vmem_limit_bytes=SMALL),
        cost_estimate=pl.CostEstimate(
            flops=2 * max(count, 256) * width * half * experts,
            bytes_accessed=2 * experts * width * half if load else 0,
            transcendentals=0,
        ),
        name="down_load" if load else "down",
    )(*operands)


def pair_shards(tokens, route_ids, route_scores, w_gate, w_up, w_down):
    groups = lax.axis_size("expert")
    local_experts = w_gate.shape[0]
    count, width = tokens.shape
    chips = groups // CORES
    here = lax.axis_index("expert").reshape(1)
    mine = lax.axis_index("tensor").reshape(1)
    other = 1 - mine
    bf16, f32 = jnp.bfloat16, jnp.float32

    def swap_tensor(value):
        return lax.ppermute(value, "tensor", [(0, 1), (1, 0)])

    def swap_expert(value, mask):
        return lax.ppermute(value, "expert", [(i, i ^ mask) for i in range(groups)])

    own = prepare(tokens, route_ids, route_scores)
    steps = [0] + list(range(chips - 1, 0, -1))
    chunks = []
    for step in steps:
        same = swap_expert(own, CORES * step) if step else own
        chunks.append(jnp.concatenate([same, swap_expert(same, 1)], axis=0))
    total = len(chunks)

    gate_other, up_other = gate_up_load(other, own, w_gate, w_up, [])
    theirs, received, kept, hidden, arrived, begun, outs = {}, {}, {}, {}, {}, {}, {}

    def send_theirs(i, after):
        theirs[i] = gate_up(chunks[i], gate_other, up_other, bf16, after)
        received[i] = swap_tensor(theirs[i])
        return [theirs[i]]

    def send_hidden(i, after):
        hidden[i] = hidden_of(here, chunks[i], kept[i], received[i], local_experts, after)
        arrived[i] = swap_tensor(hidden[i])
        return [hidden[i]]

    after = send_theirs(0, [])
    kept[0], gate_mine, up_mine = gate_up_load(mine, chunks[0], w_gate, w_up, after, f32)
    after = [kept[0]]
    for i in range(total):
        if i + 1 < total:
            after = send_theirs(i + 1, after)
        after = send_hidden(i, after)
        if i:
            outs[i - 1] = down(arrived[i - 1], begun[i - 1], bf16, after, **late)
            if i == 1:
                outs[0], down_other = outs[0]
                late = dict(held=down_other)
            after = [outs[i - 1]]
        early = dict(held=down_mine) if i else dict(side=mine, weight=w_down)
        begun[i] = down(hidden[i], None, f32, after, **early)
        if i == 0:
            begun[0], down_mine = begun[0]
            late = dict(side=other, weight=w_down)
        after = [begun[i]]
        if i + 1 < total:
            kept[i + 1] = gate_up(chunks[i + 1], gate_mine, up_mine, f32, after)
            after = [kept[i + 1]]
    outs[total - 1] = down(arrived[total - 1], begun[total - 1], bf16, after, **late)
    result = None
    for i, step in enumerate(steps):
        from_core = swap_expert(outs[i][count:], 1)
        part = outs[i][:count].astype(f32) + from_core.astype(f32)
        if step:
            part = swap_expert(part.astype(bf16), CORES * step).astype(f32)
        result = part if result is None else result + part
    return result.astype(bf16)


def solution(mesh):
    groups = mesh.shape["expert"]
    paired = mesh.shape["tensor"] == 2 and groups % CORES == 0 and groups & (groups - 1) == 0
    placed = (
        P(("replica", "expert"), "tensor"),
        P(("replica", "expert"), None),
        P(("replica", "expert"), None),
        P("expert", "tensor", None),
        P("expert", "tensor", None),
        P("expert", None, "tensor"),
    )
    return jax.shard_map(
        pair_shards if paired else general_shards,
        mesh=mesh,
        in_specs=placed,
        out_specs=P(("replica", "expert"), "tensor"),
        check_vma=False,
    )
```

```python
import functools

import jax
import jax.numpy as jnp
from jax import lax
from jax.experimental import pallas as pl
from jax.experimental.pallas import tpu as pltpu
from jax.sharding import PartitionSpec as P

CORES = 2
EXTRA = 128
SMALL = 6 * 1024 * 1024
VMEM_SPEC = pl.BlockSpec(memory_space=pltpu.VMEM)
SMEM_SPEC = pl.BlockSpec(memory_space=pltpu.SMEM)
ANY_SPEC = pl.BlockSpec(memory_space=pl.ANY)


def in_hbm(value):
    return pltpu.with_memory_space_constraint(value, pltpu.HBM)


def in_vmem(value):
    return pltpu.with_memory_space_constraint(value, pltpu.VMEM)


def slot_targets(chosen_ids, total_experts, capacity):
    expert_range = jnp.arange(total_experts, dtype=jnp.int32)
    hit_count = jnp.sum(
        (chosen_ids[:, :, None] == expert_range[None, None, :]).astype(jnp.int32), axis=1
    )
    before = jnp.cumsum(hit_count, axis=0) - hit_count
    return chosen_ids * capacity + jnp.take_along_axis(before, chosen_ids, axis=1)


def general_shards(tokens, route_ids, route_scores, w_gate, w_up, w_down):
    groups = lax.axis_size("expert")
    local_experts = w_gate.shape[0]
    count_rows = route_ids.shape[0]
    top_count = route_ids.shape[1]
    total_experts = groups * local_experts
    capacity = min(count_rows, 2 * count_rows * top_count // total_experts)
    slot_count = total_experts * capacity
    weights = route_scores / jnp.sum(route_scores, axis=1, keepdims=True)
    targets = slot_targets(route_ids, total_experts, capacity)
    row_width = tokens.shape[1]
    row_owner = jnp.broadcast_to(
        jnp.arange(count_rows, dtype=jnp.int32)[:, None], targets.shape
    ).reshape(-1)
    flat_index = targets.reshape(-1)
    source_row = jnp.zeros((slot_count,), jnp.int32).at[flat_index].set(row_owner)
    filled = jnp.zeros((slot_count,), jnp.bfloat16).at[flat_index].set(1.0)
    outgoing = (jnp.take(tokens, source_row, axis=0) * filled[:, None]).reshape(
        groups, local_experts, capacity, row_width
    )
    received = lax.all_to_all(outgoing, "expert", split_axis=0, concat_axis=0, tiled=True)
    gate_part = jnp.einsum("necd,edh->nech", received, w_gate, preferred_element_type=jnp.float32)
    up_part = jnp.einsum("necd,edh->nech", received, w_up, preferred_element_type=jnp.float32)
    gate_full, up_full = lax.psum((gate_part, up_part), "tensor")
    hidden = (jax.nn.silu(gate_full) * up_full).astype(jnp.bfloat16)
    produced = jnp.einsum("nech,ehd->necd", hidden, w_down, preferred_element_type=jnp.float32)
    returned = lax.all_to_all(produced, "expert", split_axis=0, concat_axis=0, tiled=True)
    returned = returned.reshape(slot_count, returned.shape[3])
    picked = jnp.take(returned, targets, axis=0)
    combined = jnp.sum(weights[:, :, None] * picked, axis=1)
    return combined.astype(jnp.bfloat16)


def prepare_kernel(tokens_ref, ids_ref, scores_ref, out_ref):
    count, width = tokens_ref.shape
    top = ids_ref.shape[0]
    scores = scores_ref[...]
    weights = scores / jnp.sum(scores, axis=0, keepdims=True)
    place = lax.broadcasted_iota(jnp.int32, (EXTRA, count), 0)
    share = jnp.zeros((EXTRA, count), jnp.float32)
    for k in range(top):
        chosen = ids_ref[k : k + 1, :]
        match = (place == chosen) | (place == chosen + EXTRA // 2)
        share = share + jnp.where(match, weights[k : k + 1, :], 0.0)
    high = share.astype(jnp.bfloat16).astype(jnp.float32)
    out_ref[:, :width] = tokens_ref[...]
    out_ref[:, width:] = jnp.where(place < EXTRA // 2, high, share - high).T.astype(jnp.bfloat16)


def prepare(tokens, ids, scores):
    count, width = tokens.shape
    return pl.pallas_call(
        prepare_kernel,
        in_specs=[VMEM_SPEC] * 3,
        out_specs=VMEM_SPEC,
        out_shape=jax.ShapeDtypeStruct((count, width + EXTRA), jnp.bfloat16),
        compiler_params=pltpu.CompilerParams(vmem_limit_bytes=SMALL),
        name="prepare",
    )(in_hbm(tokens), in_hbm(ids.T), in_hbm(scores.T))


def project(rows_ref, held, out_ref, expert, which, start, size):
    width, half = held.shape[1:]
    place = (2 * expert + which) * half + start
    out_ref[:, place : place + size] = jnp.dot(
        rows_ref[:, :width], held[expert, :, start : start + size], preferred_element_type=jnp.float32
    ).astype(out_ref.dtype)


def gate_up_load_kernel(compute, side_ref, rows_ref, gate_ref, up_ref, *refs):
    gate_held, up_held, sem = refs[-3:]
    experts, _, half = gate_held.shape
    tile = half // 2
    base = side_ref[0] * half
    work = []
    for e in range(experts):
        for which, source, held in ((0, gate_ref, gate_held), (1, up_ref, up_held)):
            for start in range(0, half, tile):
                copy = pltpu.make_async_copy(
                    source.at[e, :, pl.ds(pl.multiple_of(base + start, 128), tile)],
                    held.at[e, :, pl.ds(start, tile)],
                    sem.at[len(work)],
                )
                copy.start()
                work.append((copy, held, e, which, start))
    for copy, held, e, which, start in work:
        copy.wait()
        if compute:
            project(rows_ref, held, refs[-4], e, which, start, tile)


def gate_up_load(side, rows, w_gate, w_up, after, dtype=None):
    count = rows.shape[0]
    experts, width, units = w_gate.shape
    half = units // 2
    compute = dtype is not None
    held = pltpu.VMEM((experts, width, half), w_gate.dtype)
    out = [jax.ShapeDtypeStruct((count, 2 * experts * half), dtype)] if compute else []
    return pl.pallas_call(
        functools.partial(gate_up_load_kernel, compute),
        in_specs=[SMEM_SPEC, VMEM_SPEC if compute else ANY_SPEC] + [ANY_SPEC] * (2 + len(after)),
        out_specs=[VMEM_SPEC] * (2 + len(out)),
        out_shape=out + [held, held],
        scratch_shapes=[pltpu.SemaphoreType.DMA((4 * experts,))],
        compiler_params=pltpu.CompilerParams(vmem_limit_bytes=SMALL),
        cost_estimate=pl.CostEstimate(
            flops=4 * count * width * half * experts,
            bytes_accessed=4 * experts * width * half,
            transcendentals=0,
        ),
        name="gate_up_load",
    )(side, rows, in_hbm(w_gate), in_hbm(w_up), *after)


def down_copies(side_ref, weight_ref, held, sem):
    experts, half, width = held.shape
    base = pl.multiple_of(side_ref[0] * half, 256)
    return [
        pltpu.make_async_copy(weight_ref.at[e, pl.ds(base, half), :], held.at[e], sem.at[e])
        for e in range(experts)
    ]


def gate_up_kernel(load, rows_ref, gate_held, up_held, *refs):
    experts, _, half = gate_held.shape
    tile = half // 3
    copies = []
    if load:
        out_ref, held, sem = refs[-3:]
        copies = down_copies(refs[0], refs[1], held, sem)
    else:
        out_ref = refs[-1]
    for copy in copies:
        copy.start()
    for e in range(experts):
        for which, held in ((0, gate_held), (1, up_held)):
            for start in range(0, half, tile):
                project(rows_ref, held, out_ref, e, which, start, tile)
    for copy in copies:
        copy.wait()


def gate_up(rows, gate_held, up_held, dtype, after, side=None, w_down=None):
    count = rows.shape[0]
    experts, width, half = gate_held.shape
    load = w_down is not None
    out = jax.ShapeDtypeStruct((count, 2 * experts * half), dtype)
    operands = [rows, in_vmem(gate_held), in_vmem(up_held)]
    specs = [VMEM_SPEC] * 3
    if load:
        operands += [side, in_hbm(w_down)]
        specs += [SMEM_SPEC, ANY_SPEC]
    return pl.pallas_call(
        functools.partial(gate_up_kernel, load),
        in_specs=specs + [ANY_SPEC] * len(after),
        out_specs=[VMEM_SPEC] * 2 if load else VMEM_SPEC,
        out_shape=[out, pltpu.VMEM((experts, half, w_down.shape[2]), w_down.dtype)] if load else out,
        scratch_shapes=[pltpu.SemaphoreType.DMA((experts,))] if load else [],
        compiler_params=pltpu.CompilerParams(vmem_limit_bytes=SMALL),
        cost_estimate=pl.CostEstimate(
            flops=4 * max(count, 256) * width * half * experts,
            bytes_accessed=0,
            transcendentals=0,
        ),
        name="gate_up",
    )(*operands, *after)


def hidden_kernel(experts, here_ref, rows_ref, kept_ref, received_ref, *refs):
    out_ref = refs[-1]
    count = rows_ref.shape[0]
    half = kept_ref.shape[1] // (2 * experts)
    width = rows_ref.shape[1] - EXTRA
    share = rows_ref[:, width:].astype(jnp.float32)
    lane = lax.broadcasted_iota(jnp.int32, (count, EXTRA), 1)

    def full(index):
        columns = slice(index * half, (index + 1) * half)
        return kept_ref[:, columns] + received_ref[:, columns].astype(jnp.float32)

    for e in range(experts):
        expert = here_ref[0] * experts + e
        match = (lane == expert) | (lane == expert + EXTRA // 2)
        own = jnp.sum(jnp.where(match, share, 0.0), axis=1, keepdims=True)
        gate, up = full(2 * e), full(2 * e + 1)
        value = gate / (1.0 + jnp.exp(-gate)) * up * own
        out_ref[:, e * half : (e + 1) * half] = value.astype(out_ref.dtype)


def hidden_of(here, rows, kept, received, experts, after):
    count = kept.shape[0]
    half = kept.shape[1] // (2 * experts)
    return pl.pallas_call(
        functools.partial(hidden_kernel, experts),
        in_specs=[SMEM_SPEC] + [VMEM_SPEC] * 3 + [ANY_SPEC] * len(after),
        out_specs=VMEM_SPEC,
        out_shape=jax.ShapeDtypeStruct((count, experts * half), jnp.bfloat16),
        compiler_params=pltpu.CompilerParams(vmem_limit_bytes=SMALL),
        cost_estimate=pl.CostEstimate(
            flops=8 * count * half * experts,
            bytes_accessed=0,
            transcendentals=count * half * experts,
        ),
        name="hidden",
    )(here, rows, kept, received, *after)


def down_kernel(more, hidden_ref, held, *refs):
    out_ref = refs[-1]
    experts, half, width = held.shape
    tile = width // 4
    for index in range(4):
        columns = slice(index * tile, (index + 1) * tile)
        value = refs[0][:, columns] if more else None
        for e in range(experts):
            product = jnp.dot(
                hidden_ref[:, e * half : (e + 1) * half],
                held[e, :, columns],
                preferred_element_type=jnp.float32,
            )
            value = product if value is None else value + product
        out_ref[:, columns] = value


def down(hidden, held, so_far, after):
    count = hidden.shape[0]
    experts, half, width = held.shape
    extra = [] if so_far is None else [so_far]
    return pl.pallas_call(
        functools.partial(down_kernel, len(extra)),
        in_specs=[VMEM_SPEC] * (2 + len(extra)) + [ANY_SPEC] * len(after),
        out_specs=VMEM_SPEC,
        out_shape=jax.ShapeDtypeStruct((count, width), jnp.float32),
        compiler_params=pltpu.CompilerParams(vmem_limit_bytes=SMALL),
        cost_estimate=pl.CostEstimate(
            flops=2 * max(count, 256) * width * half * experts,
            bytes_accessed=0,
            transcendentals=0,
        ),
        name="down",
    )(hidden, in_vmem(held), *extra, *after)


def pair_shards(tokens, route_ids, route_scores, w_gate, w_up, w_down):
    groups = lax.axis_size("expert")
    local_experts = w_gate.shape[0]
    count = tokens.shape[0]
    chips = groups // CORES
    here = lax.axis_index("expert").reshape(1)
    mine = lax.axis_index("tensor").reshape(1)
    other = 1 - mine
    bf16, f32 = jnp.bfloat16, jnp.float32

    def swap_tensor(value):
        return lax.ppermute(value, "tensor", [(0, 1), (1, 0)])

    def swap_expert(value, mask):
        return lax.ppermute(value, "expert", [(i, i ^ mask) for i in range(groups)])

    def later(value, than):
        return lax.optimization_barrier((value, than))[0]

    near, far = CORES, [CORES * step for step in range(chips - 1, 1, -1)]
    fills = [-count % 8] + [-(CORES * count) % 8] * len(far) + [-count % 8]
    first = (count - sum(fills[:2])) // 8 * 8
    if CORES * count - first - sum(fills) < 8:
        fills = [0] * len(fills)
    begins = [first + sum(fills[:i]) for i in range(len(fills) + 1)]
    last = len(fills) + 1

    own = prepare(tokens, route_ids, route_scores)
    near_same = swap_expert(own, near)
    came = [swap_expert(own, mask) for mask in far[:1]]
    theirs, received, kept, hidden, arrived, begun, outs, chunks = {}, {}, {}, {}, {}, {}, {}, {}
    parts, back, after = {}, [], []

    def local(begin, end):
        if end <= count:
            return [own[begin:end]]
        if begin >= count:
            return [partner[begin - count : end - count]]
        return [own[begin:], partner[: end - count]]

    def bring(i, rows):
        chunks[i] = jnp.concatenate(rows + local(begins[i - 1], begins[i]), axis=0)

    def bring_far(i):
        rows = later(came[i - 2], after[0])
        bring(i, [rows, swap_expert(rows, 1)])

    def send_theirs(i, **load):
        theirs[i] = gate_up(chunks[i], gate_other, up_other, bf16, after, **load)
        more = []
        if load:
            theirs[i], *more = theirs[i]
        received[i] = swap_tensor(theirs[i])
        after[:] = [theirs[i]]
        return more

    def keep(i, **load):
        kept[i] = gate_up(chunks[i], gate_mine, up_mine, f32, after, **load)
        more = []
        if load:
            kept[i], *more = kept[i]
        after[:] = [kept[i]]
        return more

    def send_hidden(i):
        hidden[i] = hidden_of(here, chunks[i], kept[i], received[i], local_experts, after)
        arrived[i] = swap_tensor(hidden[i])
        after[:] = [hidden[i]]

    def begin_down(i):
        begun[i] = down(hidden[i], down_mine, None, after)
        after[:] = [begun[i]]

    def end_down(i):
        out = outs[i] = down(arrived[i], down_other, begun[i], after)
        after[:] = [out]
        if i in (1, last - 1):
            back.append(swap_expert(out[:count].astype(bf16), near + (i != 1)))
        elif 1 < i < last:
            from_core = swap_expert(out[count : CORES * count].astype(bf16), 1)
            parts[i] = (out[:count] + from_core.astype(f32)).astype(bf16)
            back.append(swap_expert(parts[i], far[i - 2]))

    chunks[0] = own[:first]
    theirs[0], gate_other, up_other = gate_up_load(other, chunks[0], w_gate, w_up, [here, mine], bf16)
    received[0] = swap_tensor(theirs[0])
    after[:] = [theirs[0]]
    bring(1, [near_same])
    send_theirs(1)
    waiting = later(own, theirs[1])
    partner = swap_expert(waiting, 1)
    came += [swap_expert(waiting, mask) for mask in far[1:]]
    kept[0], gate_mine, up_mine = gate_up_load(mine, chunks[0], w_gate, w_up, after, f32)
    after[:] = [kept[0]]
    send_hidden(0)
    if far:
        bring_far(2)
    keep(1)
    send_hidden(1)
    near_other = swap_expert(later(own, hidden[1]), near + 1)
    if not far:
        bring(2, [near_other])
    (down_mine,) = send_theirs(2, side=mine, w_down=w_down)
    if len(far) > 1:
        bring_far(3)
    elif far:
        bring(3, [near_other])
    else:
        chunks[3] = partner[begins[-1] - count :]
    (down_other,) = keep(2, side=other, w_down=w_down)
    begin_down(0)
    send_theirs(3)
    begin_down(1)
    for i in range(2, last + 1):
        send_hidden(i)
        if i + 2 <= last:
            if i + 2 == last:
                chunks[last] = partner[begins[-1] - count :]
            elif i + 2 == last - 1:
                bring(i + 2, [later(near_other, hidden[i])])
            else:
                bring_far(i + 2)
            send_theirs(i + 2)
        for early in (0, 1) if i == 2 else (i - 1,):
            end_down(early)
        begin_down(i)
        if i < last:
            keep(i + 1)
        if i - 1 in parts:
            after.append(parts[i - 1])
    end_down(last)

    pieces = [outs[0]]
    for i in range(1, last):
        pieces.append(outs[i][count if i in (1, last - 1) else CORES * count :])
    pieces = jnp.concatenate(pieces + [outs[last]], axis=0)
    from_core = swap_expert(pieces[count:].astype(bf16), 1)
    result = pieces[:count]
    for value in back + [from_core]:
        result = result + value.astype(f32)
    return result.astype(bf16)


def solution(mesh):
    groups = mesh.shape["expert"]
    paired = mesh.shape["tensor"] == 2 and groups > CORES and groups & (groups - 1) == 0
    placed = (
        P(("replica", "expert"), "tensor"),
        P(("replica", "expert"), None),
        P(("replica", "expert"), None),
        P("expert", "tensor", None),
        P("expert", "tensor", None),
        P("expert", None, "tensor"),
    )
    return jax.shard_map(
        pair_shards if paired else general_shards,
        mesh=mesh,
        in_specs=placed,
        out_specs=P(("replica", "expert"), "tensor"),
        check_vma=False,
    )
```

```python
import functools

import jax
import jax.numpy as jnp
from jax import lax
from jax.experimental import pallas as pl
from jax.experimental.pallas import tpu as pltpu
from jax.sharding import PartitionSpec as P

CORES = 2
EXTRA = 128
SMALL = 6 * 1024 * 1024
VMEM_SPEC = pl.BlockSpec(memory_space=pltpu.VMEM)
SMEM_SPEC = pl.BlockSpec(memory_space=pltpu.SMEM)
ANY_SPEC = pl.BlockSpec(memory_space=pl.ANY)


def in_hbm(value):
    return pltpu.with_memory_space_constraint(value, pltpu.HBM)


def in_vmem(value):
    return pltpu.with_memory_space_constraint(value, pltpu.VMEM)


def slot_targets(chosen_ids, total_experts, capacity):
    expert_range = jnp.arange(total_experts, dtype=jnp.int32)
    hit_count = jnp.sum(
        (chosen_ids[:, :, None] == expert_range[None, None, :]).astype(jnp.int32), axis=1
    )
    before = jnp.cumsum(hit_count, axis=0) - hit_count
    return chosen_ids * capacity + jnp.take_along_axis(before, chosen_ids, axis=1)


def general_shards(tokens, route_ids, route_scores, w_gate, w_up, w_down):
    groups = lax.axis_size("expert")
    local_experts = w_gate.shape[0]
    count_rows = route_ids.shape[0]
    top_count = route_ids.shape[1]
    total_experts = groups * local_experts
    capacity = min(count_rows, 2 * count_rows * top_count // total_experts)
    slot_count = total_experts * capacity
    weights = route_scores / jnp.sum(route_scores, axis=1, keepdims=True)
    targets = slot_targets(route_ids, total_experts, capacity)
    row_width = tokens.shape[1]
    row_owner = jnp.broadcast_to(
        jnp.arange(count_rows, dtype=jnp.int32)[:, None], targets.shape
    ).reshape(-1)
    flat_index = targets.reshape(-1)
    source_row = jnp.zeros((slot_count,), jnp.int32).at[flat_index].set(row_owner)
    filled = jnp.zeros((slot_count,), jnp.bfloat16).at[flat_index].set(1.0)
    outgoing = (jnp.take(tokens, source_row, axis=0) * filled[:, None]).reshape(
        groups, local_experts, capacity, row_width
    )
    received = lax.all_to_all(outgoing, "expert", split_axis=0, concat_axis=0, tiled=True)
    gate_part = jnp.einsum("necd,edh->nech", received, w_gate, preferred_element_type=jnp.float32)
    up_part = jnp.einsum("necd,edh->nech", received, w_up, preferred_element_type=jnp.float32)
    gate_full, up_full = lax.psum((gate_part, up_part), "tensor")
    hidden = (jax.nn.silu(gate_full) * up_full).astype(jnp.bfloat16)
    produced = jnp.einsum("nech,ehd->necd", hidden, w_down, preferred_element_type=jnp.float32)
    returned = lax.all_to_all(produced, "expert", split_axis=0, concat_axis=0, tiled=True)
    returned = returned.reshape(slot_count, returned.shape[3])
    picked = jnp.take(returned, targets, axis=0)
    combined = jnp.sum(weights[:, :, None] * picked, axis=1)
    return combined.astype(jnp.bfloat16)


def prepare_kernel(tokens_ref, ids_ref, scores_ref, out_ref):
    count, width = tokens_ref.shape
    top = ids_ref.shape[0]
    scores = scores_ref[...]
    weights = scores / jnp.sum(scores, axis=0, keepdims=True)
    place = lax.broadcasted_iota(jnp.int32, (EXTRA, count), 0)
    share = jnp.zeros((EXTRA, count), jnp.float32)
    for k in range(top):
        chosen = ids_ref[k : k + 1, :]
        match = (place == chosen) | (place == chosen + EXTRA // 2)
        share = share + jnp.where(match, weights[k : k + 1, :], 0.0)
    high = share.astype(jnp.bfloat16).astype(jnp.float32)
    out_ref[:, :width] = tokens_ref[...]
    out_ref[:, width:] = jnp.where(place < EXTRA // 2, high, share - high).T.astype(jnp.bfloat16)


def prepare(tokens, ids, scores):
    count, width = tokens.shape
    return pl.pallas_call(
        prepare_kernel,
        in_specs=[VMEM_SPEC] * 3,
        out_specs=VMEM_SPEC,
        out_shape=jax.ShapeDtypeStruct((count, width + EXTRA), jnp.bfloat16),
        compiler_params=pltpu.CompilerParams(vmem_limit_bytes=SMALL),
        name="prepare",
    )(in_hbm(tokens), in_hbm(ids.T), in_hbm(scores.T))


def project(rows_ref, held, out_ref, expert, which, start, size):
    width, half = held.shape[1:]
    place = (2 * expert + which) * half + start
    out_ref[:, place : place + size] = jnp.dot(
        rows_ref[:, :width], held[expert, :, start : start + size], preferred_element_type=jnp.float32
    ).astype(out_ref.dtype)


def gate_up_load_kernel(compute, side_ref, rows_ref, gate_ref, up_ref, *refs):
    gate_held, up_held, sem = refs[-3:]
    experts, _, half = gate_held.shape
    tile = half // 2
    base = side_ref[0] * half
    work = []
    for e in range(experts):
        for which, source, held in ((0, gate_ref, gate_held), (1, up_ref, up_held)):
            for start in range(0, half, tile):
                copy = pltpu.make_async_copy(
                    source.at[e, :, pl.ds(pl.multiple_of(base + start, 128), tile)],
                    held.at[e, :, pl.ds(start, tile)],
                    sem.at[len(work)],
                )
                copy.start()
                work.append((copy, held, e, which, start))
    for copy, held, e, which, start in work:
        copy.wait()
        if compute:
            project(rows_ref, held, refs[-4], e, which, start, tile)


def gate_up_load(side, rows, w_gate, w_up, after, dtype=None):
    count = rows.shape[0]
    experts, width, units = w_gate.shape
    half = units // 2
    compute = dtype is not None
    held = pltpu.VMEM((experts, width, half), w_gate.dtype)
    out = [jax.ShapeDtypeStruct((count, 2 * experts * half), dtype)] if compute else []
    return pl.pallas_call(
        functools.partial(gate_up_load_kernel, compute),
        in_specs=[SMEM_SPEC, VMEM_SPEC if compute else ANY_SPEC] + [ANY_SPEC] * (2 + len(after)),
        out_specs=[VMEM_SPEC] * (2 + len(out)),
        out_shape=out + [held, held],
        scratch_shapes=[pltpu.SemaphoreType.DMA((4 * experts,))],
        compiler_params=pltpu.CompilerParams(vmem_limit_bytes=SMALL),
        cost_estimate=pl.CostEstimate(
            flops=4 * count * width * half * experts,
            bytes_accessed=4 * experts * width * half,
            transcendentals=0,
        ),
        name="gate_up_load",
    )(side, rows, in_hbm(w_gate), in_hbm(w_up), *after)


def down_copies(side_ref, weight_ref, held, sem):
    experts, half, width = held.shape
    base = pl.multiple_of(side_ref[0] * half, 256)
    return [
        pltpu.make_async_copy(weight_ref.at[e, pl.ds(base, half), :], held.at[e], sem.at[e])
        for e in range(experts)
    ]


def gate_up_kernel(load, rows_ref, gate_held, up_held, *refs):
    experts, _, half = gate_held.shape
    tile = half // 3
    copies = []
    if load:
        out_ref, held, sem = refs[-3:]
        copies = down_copies(refs[0], refs[1], held, sem)
    else:
        out_ref = refs[-1]
    for copy in copies:
        copy.start()
    for e in range(experts):
        for which, held in ((0, gate_held), (1, up_held)):
            for start in range(0, half, tile):
                project(rows_ref, held, out_ref, e, which, start, tile)
    for copy in copies:
        copy.wait()


def gate_up(rows, gate_held, up_held, dtype, after, side=None, w_down=None):
    count = rows.shape[0]
    experts, width, half = gate_held.shape
    load = w_down is not None
    out = jax.ShapeDtypeStruct((count, 2 * experts * half), dtype)
    operands = [rows, in_vmem(gate_held), in_vmem(up_held)]
    specs = [VMEM_SPEC] * 3
    if load:
        operands += [side, in_hbm(w_down)]
        specs += [SMEM_SPEC, ANY_SPEC]
    return pl.pallas_call(
        functools.partial(gate_up_kernel, load),
        in_specs=specs + [ANY_SPEC] * len(after),
        out_specs=[VMEM_SPEC] * 2 if load else VMEM_SPEC,
        out_shape=[out, pltpu.VMEM((experts, half, w_down.shape[2]), w_down.dtype)] if load else out,
        scratch_shapes=[pltpu.SemaphoreType.DMA((experts,))] if load else [],
        compiler_params=pltpu.CompilerParams(vmem_limit_bytes=SMALL),
        cost_estimate=pl.CostEstimate(
            flops=4 * max(count, 256) * width * half * experts,
            bytes_accessed=0,
            transcendentals=0,
        ),
        name="gate_up",
    )(*operands, *after)


def hidden_kernel(experts, here_ref, rows_ref, kept_ref, received_ref, *refs):
    out_ref = refs[-1]
    count = rows_ref.shape[0]
    half = kept_ref.shape[1] // (2 * experts)
    width = rows_ref.shape[1] - EXTRA
    share = rows_ref[:, width:].astype(jnp.float32)
    lane = lax.broadcasted_iota(jnp.int32, (count, EXTRA), 1)

    def full(index):
        columns = slice(index * half, (index + 1) * half)
        return kept_ref[:, columns] + received_ref[:, columns].astype(jnp.float32)

    for e in range(experts):
        expert = here_ref[0] * experts + e
        match = (lane == expert) | (lane == expert + EXTRA // 2)
        own = jnp.sum(jnp.where(match, share, 0.0), axis=1, keepdims=True)
        gate, up = full(2 * e), full(2 * e + 1)
        value = gate / (1.0 + jnp.exp(-gate)) * up * own
        out_ref[:, e * half : (e + 1) * half] = value.astype(out_ref.dtype)


def hidden_of(here, rows, kept, received, experts, after):
    count = kept.shape[0]
    half = kept.shape[1] // (2 * experts)
    return pl.pallas_call(
        functools.partial(hidden_kernel, experts),
        in_specs=[SMEM_SPEC] + [VMEM_SPEC] * 3 + [ANY_SPEC] * len(after),
        out_specs=VMEM_SPEC,
        out_shape=jax.ShapeDtypeStruct((count, experts * half), jnp.bfloat16),
        compiler_params=pltpu.CompilerParams(vmem_limit_bytes=SMALL),
        cost_estimate=pl.CostEstimate(
            flops=8 * count * half * experts,
            bytes_accessed=0,
            transcendentals=count * half * experts,
        ),
        name="hidden",
    )(here, rows, kept, received, *after)


def down_kernel(more, hidden_ref, held, *refs):
    out_ref = refs[-1]
    experts, half, width = held.shape
    tile = width // 4
    for index in range(4):
        columns = slice(index * tile, (index + 1) * tile)
        value = refs[0][:, columns] if more else None
        for e in range(experts):
            product = jnp.dot(
                hidden_ref[:, e * half : (e + 1) * half],
                held[e, :, columns],
                preferred_element_type=jnp.float32,
            )
            value = product if value is None else value + product
        out_ref[:, columns] = value


def down(hidden, held, so_far, after, weight=1):
    count = hidden.shape[0]
    experts, half, width = held.shape
    extra = [] if so_far is None else [so_far]
    return pl.pallas_call(
        functools.partial(down_kernel, len(extra)),
        in_specs=[VMEM_SPEC] * (2 + len(extra)) + [ANY_SPEC] * len(after),
        out_specs=VMEM_SPEC,
        out_shape=jax.ShapeDtypeStruct((count, width), jnp.float32),
        compiler_params=pltpu.CompilerParams(vmem_limit_bytes=SMALL),
        cost_estimate=pl.CostEstimate(
            flops=weight * 2 * max(count, 256) * width * half * experts,
            bytes_accessed=0,
            transcendentals=0,
        ),
        name="down",
    )(hidden, in_vmem(held), *extra, *after)


def pair_shards(tokens, route_ids, route_scores, w_gate, w_up, w_down):
    groups = lax.axis_size("expert")
    local_experts = w_gate.shape[0]
    count = tokens.shape[0]
    chips = groups // CORES
    here = lax.axis_index("expert").reshape(1)
    mine = lax.axis_index("tensor").reshape(1)
    other = 1 - mine
    bf16, f32 = jnp.bfloat16, jnp.float32

    def swap_tensor(value):
        return lax.ppermute(value, "tensor", [(0, 1), (1, 0)])

    def swap_expert(value, mask):
        return lax.ppermute(value, "expert", [(i, i ^ mask) for i in range(groups)])

    def later(value, than):
        return lax.optimization_barrier((value, than))[0]

    near, far = CORES, [CORES * step for step in range(chips - 1, 1, -1)]
    fills = [-count % 8] + [-(CORES * count) % 8] * len(far) + [-count % 8]
    first = (count - sum(fills[:2])) // 8 * 8
    if CORES * count - first - sum(fills) < 8:
        fills = [0] * len(fills)
    begins = [first + sum(fills[:i]) for i in range(len(fills) + 1)]
    last = len(fills) + 1

    own = prepare(tokens, route_ids, route_scores)
    near_same = swap_expert(own, near)
    came = [swap_expert(own, mask) for mask in far]
    theirs, received, kept, hidden, arrived, begun, outs, chunks = {}, {}, {}, {}, {}, {}, {}, {}
    parts, back, after = {}, [], []

    def local(begin, end):
        if end <= count:
            return [own[begin:end]]
        if begin >= count:
            return [partner[begin - count : end - count]]
        return [own[begin:], partner[: end - count]]

    def bring(i, rows):
        chunks[i] = jnp.concatenate(rows + local(begins[i - 1], begins[i]), axis=0)

    def bring_far(i):
        rows = later(came[i - 2], after[0])
        bring(i, [rows, swap_expert(rows, 1)])

    def send_theirs(i, **load):
        theirs[i] = gate_up(chunks[i], gate_other, up_other, bf16, after, **load)
        more = []
        if load:
            theirs[i], *more = theirs[i]
        received[i] = swap_tensor(theirs[i])
        after[:] = [theirs[i]]
        return more

    def keep(i, **load):
        kept[i] = gate_up(chunks[i], gate_mine, up_mine, f32, after, **load)
        more = []
        if load:
            kept[i], *more = kept[i]
        after[:] = [kept[i]]
        return more

    def send_hidden(i):
        hidden[i] = hidden_of(here, chunks[i], kept[i], received[i], local_experts, after)
        arrived[i] = swap_tensor(hidden[i])
        after[:] = [hidden[i]]

    def begin_down(i):
        begun[i] = down(hidden[i], down_mine, None, after, 3 if i == last - 1 else 1)
        after[:] = [begun[i]]

    def end_down(i):
        out = outs[i] = down(arrived[i], down_other, begun[i], after)
        after[:] = [out]
        if i in (1, last - 1):
            back.append(swap_expert(out[:count].astype(bf16), near + (i != 1)))
        elif 1 < i < last:
            from_core = swap_expert(out[count : CORES * count].astype(bf16), 1)
            parts[i] = (out[:count] + from_core.astype(f32)).astype(bf16)
            back.append(swap_expert(parts[i], far[i - 2]))

    chunks[0] = own[:first]
    theirs[0], gate_other, up_other = gate_up_load(other, chunks[0], w_gate, w_up, [here, mine], bf16)
    received[0] = swap_tensor(theirs[0])
    after[:] = [theirs[0]]
    bring(1, [near_same])
    send_theirs(1)
    kept[0], gate_mine, up_mine = gate_up_load(mine, chunks[0], w_gate, w_up, after, f32)
    after[:] = [kept[0]]
    partner = swap_expert(later(own, kept[0]), 1)
    send_hidden(0)
    if far:
        bring_far(2)
    keep(1)
    send_hidden(1)
    near_other = swap_expert(later(own, hidden[1]), near + 1)
    if not far:
        bring(2, [near_other])
    (down_mine,) = send_theirs(2, side=mine, w_down=w_down)
    if len(far) > 1:
        bring_far(3)
    elif far:
        bring(3, [near_other])
    else:
        chunks[3] = partner[begins[-1] - count :]
    (down_other,) = keep(2, side=other, w_down=w_down)
    begin_down(0)
    send_theirs(3)
    begin_down(1)
    for i in range(2, last + 1):
        send_hidden(i)
        if i + 2 <= last:
            if i + 2 == last:
                chunks[last] = partner[begins[-1] - count :]
            elif i + 2 == last - 1:
                bring(i + 2, [later(near_other, hidden[i])])
            else:
                bring_far(i + 2)
            send_theirs(i + 2)
        if i == last - 1:
            keep(last)
        for early in (0, 1) if i == 2 else (i - 1,):
            end_down(early)
        begin_down(i)
        if i + 1 < last:
            keep(i + 1)
        if i - 1 in parts:
            after.append(parts[i - 1])
    end_down(last)

    pieces = [outs[0]]
    for i in range(1, last):
        pieces.append(outs[i][count if i in (1, last - 1) else CORES * count :])
    pieces = jnp.concatenate(pieces + [outs[last]], axis=0)
    from_core = swap_expert(pieces[count:].astype(bf16), 1)
    result = pieces[:count]
    for value in back + [from_core]:
        result = result + value.astype(f32)
    return result.astype(bf16)


def solution(mesh):
    groups = mesh.shape["expert"]
    paired = mesh.shape["tensor"] == 2 and groups > CORES and groups & (groups - 1) == 0
    placed = (
        P(("replica", "expert"), "tensor"),
        P(("replica", "expert"), None),
        P(("replica", "expert"), None),
        P("expert", "tensor", None),
        P("expert", "tensor", None),
        P("expert", None, "tensor"),
    )
    return jax.shard_map(
        pair_shards if paired else general_shards,
        mesh=mesh,
        in_specs=placed,
        out_specs=P(("replica", "expert"), "tensor"),
        check_vma=False,
    )
```

```python
import functools

import jax
import jax.numpy as jnp
from jax import lax
from jax.experimental import pallas as pl
from jax.experimental.pallas import tpu as pltpu
from jax.sharding import PartitionSpec as P

CORES = 2
EXTRA = 128
SMALL = 6 * 1024 * 1024
VMEM_SPEC = pl.BlockSpec(memory_space=pltpu.VMEM)
SMEM_SPEC = pl.BlockSpec(memory_space=pltpu.SMEM)
ANY_SPEC = pl.BlockSpec(memory_space=pl.ANY)


def in_hbm(value):
    return pltpu.with_memory_space_constraint(value, pltpu.HBM)


def in_vmem(value):
    return pltpu.with_memory_space_constraint(value, pltpu.VMEM)


def slot_targets(chosen_ids, total_experts, capacity):
    expert_range = jnp.arange(total_experts, dtype=jnp.int32)
    hit_count = jnp.sum(
        (chosen_ids[:, :, None] == expert_range[None, None, :]).astype(jnp.int32), axis=1
    )
    before = jnp.cumsum(hit_count, axis=0) - hit_count
    return chosen_ids * capacity + jnp.take_along_axis(before, chosen_ids, axis=1)


def general_shards(tokens, route_ids, route_scores, w_gate, w_up, w_down):
    groups = lax.axis_size("expert")
    local_experts = w_gate.shape[0]
    count_rows = route_ids.shape[0]
    top_count = route_ids.shape[1]
    total_experts = groups * local_experts
    capacity = min(count_rows, 2 * count_rows * top_count // total_experts)
    slot_count = total_experts * capacity
    weights = route_scores / jnp.sum(route_scores, axis=1, keepdims=True)
    targets = slot_targets(route_ids, total_experts, capacity)
    row_width = tokens.shape[1]
    row_owner = jnp.broadcast_to(
        jnp.arange(count_rows, dtype=jnp.int32)[:, None], targets.shape
    ).reshape(-1)
    flat_index = targets.reshape(-1)
    source_row = jnp.zeros((slot_count,), jnp.int32).at[flat_index].set(row_owner)
    filled = jnp.zeros((slot_count,), jnp.bfloat16).at[flat_index].set(1.0)
    outgoing = (jnp.take(tokens, source_row, axis=0) * filled[:, None]).reshape(
        groups, local_experts, capacity, row_width
    )
    received = lax.all_to_all(outgoing, "expert", split_axis=0, concat_axis=0, tiled=True)
    gate_part = jnp.einsum("necd,edh->nech", received, w_gate, preferred_element_type=jnp.float32)
    up_part = jnp.einsum("necd,edh->nech", received, w_up, preferred_element_type=jnp.float32)
    gate_full, up_full = lax.psum((gate_part, up_part), "tensor")
    hidden = (jax.nn.silu(gate_full) * up_full).astype(jnp.bfloat16)
    produced = jnp.einsum("nech,ehd->necd", hidden, w_down, preferred_element_type=jnp.float32)
    returned = lax.all_to_all(produced, "expert", split_axis=0, concat_axis=0, tiled=True)
    returned = returned.reshape(slot_count, returned.shape[3])
    picked = jnp.take(returned, targets, axis=0)
    combined = jnp.sum(weights[:, :, None] * picked, axis=1)
    return combined.astype(jnp.bfloat16)


def prepare_kernel(tokens_ref, ids_ref, scores_ref, out_ref):
    count, width = tokens_ref.shape
    top = ids_ref.shape[0]
    scores = scores_ref[...]
    weights = scores / jnp.sum(scores, axis=0, keepdims=True)
    place = lax.broadcasted_iota(jnp.int32, (EXTRA, count), 0)
    share = jnp.zeros((EXTRA, count), jnp.float32)
    for k in range(top):
        chosen = ids_ref[k : k + 1, :]
        match = (place == chosen) | (place == chosen + EXTRA // 2)
        share = share + jnp.where(match, weights[k : k + 1, :], 0.0)
    high = share.astype(jnp.bfloat16).astype(jnp.float32)
    out_ref[:, :width] = tokens_ref[...]
    out_ref[:, width:] = jnp.where(place < EXTRA // 2, high, share - high).T.astype(jnp.bfloat16)


def prepare(tokens, ids, scores):
    count, width = tokens.shape
    return pl.pallas_call(
        prepare_kernel,
        in_specs=[VMEM_SPEC] * 3,
        out_specs=VMEM_SPEC,
        out_shape=jax.ShapeDtypeStruct((count, width + EXTRA), jnp.bfloat16),
        compiler_params=pltpu.CompilerParams(vmem_limit_bytes=SMALL),
        name="prepare",
    )(in_hbm(tokens), in_hbm(ids.T), in_hbm(scores.T))


def project(rows_ref, held, out_ref, expert, which, start, size):
    width, half = held.shape[1:]
    place = (2 * expert + which) * half + start
    out_ref[:, place : place + size] = jnp.dot(
        rows_ref[:, :width], held[expert, :, start : start + size], preferred_element_type=jnp.float32
    ).astype(out_ref.dtype)


def gate_up_load_kernel(compute, side_ref, rows_ref, gate_ref, up_ref, *refs):
    gate_held, up_held, sem = refs[-3:]
    experts, _, half = gate_held.shape
    tile = half // 2
    base = side_ref[0] * half
    work = []
    for e in range(experts):
        for which, source, held in ((0, gate_ref, gate_held), (1, up_ref, up_held)):
            for start in range(0, half, tile):
                copy = pltpu.make_async_copy(
                    source.at[e, :, pl.ds(pl.multiple_of(base + start, 128), tile)],
                    held.at[e, :, pl.ds(start, tile)],
                    sem.at[len(work)],
                )
                copy.start()
                work.append((copy, held, e, which, start))
    for copy, held, e, which, start in work:
        copy.wait()
        if compute:
            project(rows_ref, held, refs[-4], e, which, start, tile)


def gate_up_load(side, rows, w_gate, w_up, after, dtype=None):
    count = rows.shape[0]
    experts, width, units = w_gate.shape
    half = units // 2
    compute = dtype is not None
    held = pltpu.VMEM((experts, width, half), w_gate.dtype)
    out = [jax.ShapeDtypeStruct((count, 2 * experts * half), dtype)] if compute else []
    return pl.pallas_call(
        functools.partial(gate_up_load_kernel, compute),
        in_specs=[SMEM_SPEC, VMEM_SPEC if compute else ANY_SPEC] + [ANY_SPEC] * (2 + len(after)),
        out_specs=[VMEM_SPEC] * (2 + len(out)),
        out_shape=out + [held, held],
        scratch_shapes=[pltpu.SemaphoreType.DMA((4 * experts,))],
        compiler_params=pltpu.CompilerParams(vmem_limit_bytes=SMALL),
        cost_estimate=pl.CostEstimate(
            flops=4 * count * width * half * experts,
            bytes_accessed=4 * experts * width * half,
            transcendentals=0,
        ),
        name="gate_up_load",
    )(side, rows, in_hbm(w_gate), in_hbm(w_up), *after)


def down_copies(side_ref, weight_ref, held, sem):
    experts, half, width = held.shape
    base = pl.multiple_of(side_ref[0] * half, 256)
    return [
        pltpu.make_async_copy(weight_ref.at[e, pl.ds(base, half), :], held.at[e], sem.at[e])
        for e in range(experts)
    ]


def gate_up_kernel(load, rows_ref, gate_held, up_held, *refs):
    experts, _, half = gate_held.shape
    tile = half // 2
    copies = []
    if load:
        out_ref, held, sem = refs[-3:]
        copies = down_copies(refs[0], refs[1], held, sem)
    else:
        out_ref = refs[-1]
    for copy in copies:
        copy.start()
    for e in range(experts):
        for which, held in ((0, gate_held), (1, up_held)):
            for start in range(0, half, tile):
                project(rows_ref, held, out_ref, e, which, start, tile)
    for copy in copies:
        copy.wait()


def gate_up(rows, gate_held, up_held, dtype, after, side=None, w_down=None):
    count = rows.shape[0]
    experts, width, half = gate_held.shape
    load = w_down is not None
    out = jax.ShapeDtypeStruct((count, 2 * experts * half), dtype)
    operands = [rows, in_vmem(gate_held), in_vmem(up_held)]
    specs = [VMEM_SPEC] * 3
    if load:
        operands += [side, in_hbm(w_down)]
        specs += [SMEM_SPEC, ANY_SPEC]
    return pl.pallas_call(
        functools.partial(gate_up_kernel, load),
        in_specs=specs + [ANY_SPEC] * len(after),
        out_specs=[VMEM_SPEC] * 2 if load else VMEM_SPEC,
        out_shape=[out, pltpu.VMEM((experts, half, w_down.shape[2]), w_down.dtype)] if load else out,
        scratch_shapes=[pltpu.SemaphoreType.DMA((experts,))] if load else [],
        compiler_params=pltpu.CompilerParams(vmem_limit_bytes=SMALL),
        cost_estimate=pl.CostEstimate(
            flops=4 * max(count, 256) * width * half * experts,
            bytes_accessed=0,
            transcendentals=0,
        ),
        name="gate_up",
    )(*operands, *after)


def hidden_kernel(experts, here_ref, rows_ref, kept_ref, received_ref, *refs):
    out_ref = refs[-1]
    count = rows_ref.shape[0]
    half = kept_ref.shape[1] // (2 * experts)
    width = rows_ref.shape[1] - EXTRA
    share = rows_ref[:, width:].astype(jnp.float32)
    lane = lax.broadcasted_iota(jnp.int32, (count, EXTRA), 1)

    def full(index):
        columns = slice(index * half, (index + 1) * half)
        return kept_ref[:, columns] + received_ref[:, columns].astype(jnp.float32)

    for e in range(experts):
        expert = here_ref[0] * experts + e
        match = (lane == expert) | (lane == expert + EXTRA // 2)
        own = jnp.sum(jnp.where(match, share, 0.0), axis=1, keepdims=True)
        gate, up = full(2 * e), full(2 * e + 1)
        value = gate / (1.0 + jnp.exp(-gate)) * up * own
        out_ref[:, e * half : (e + 1) * half] = value.astype(out_ref.dtype)


def hidden_of(here, rows, kept, received, experts, after):
    count = kept.shape[0]
    half = kept.shape[1] // (2 * experts)
    return pl.pallas_call(
        functools.partial(hidden_kernel, experts),
        in_specs=[SMEM_SPEC] + [VMEM_SPEC] * 3 + [ANY_SPEC] * len(after),
        out_specs=VMEM_SPEC,
        out_shape=jax.ShapeDtypeStruct((count, experts * half), jnp.bfloat16),
        compiler_params=pltpu.CompilerParams(vmem_limit_bytes=SMALL),
        cost_estimate=pl.CostEstimate(
            flops=8 * count * half * experts,
            bytes_accessed=0,
            transcendentals=count * half * experts,
        ),
        name="hidden",
    )(here, rows, kept, received, *after)


def down_kernel(more, hidden_ref, held, *refs):
    out_ref = refs[-1]
    experts, half, width = held.shape
    tile = width // 4
    for index in range(4):
        columns = slice(index * tile, (index + 1) * tile)
        value = refs[0][:, columns] if more else None
        for e in range(experts):
            product = jnp.dot(
                hidden_ref[:, e * half : (e + 1) * half],
                held[e, :, columns],
                preferred_element_type=jnp.float32,
            )
            value = product if value is None else value + product
        out_ref[:, columns] = value


def down(hidden, held, so_far, after, weight=1):
    count = hidden.shape[0]
    experts, half, width = held.shape
    extra = [] if so_far is None else [so_far]
    return pl.pallas_call(
        functools.partial(down_kernel, len(extra)),
        in_specs=[VMEM_SPEC] * (2 + len(extra)) + [ANY_SPEC] * len(after),
        out_specs=VMEM_SPEC,
        out_shape=jax.ShapeDtypeStruct((count, width), jnp.float32),
        compiler_params=pltpu.CompilerParams(vmem_limit_bytes=SMALL),
        cost_estimate=pl.CostEstimate(
            flops=weight * 2 * max(count, 256) * width * half * experts,
            bytes_accessed=0,
            transcendentals=0,
        ),
        name="down",
    )(hidden, in_vmem(held), *extra, *after)


def pair_shards(tokens, route_ids, route_scores, w_gate, w_up, w_down):
    groups = lax.axis_size("expert")
    local_experts = w_gate.shape[0]
    count = tokens.shape[0]
    chips = groups // CORES
    here = lax.axis_index("expert").reshape(1)
    mine = lax.axis_index("tensor").reshape(1)
    other = 1 - mine
    bf16, f32 = jnp.bfloat16, jnp.float32

    def swap_tensor(value):
        return lax.ppermute(value, "tensor", [(0, 1), (1, 0)])

    def swap_expert(value, mask):
        return lax.ppermute(value, "expert", [(i, i ^ mask) for i in range(groups)])

    def later(value, than):
        return lax.optimization_barrier((value, than))[0]

    near, far = CORES, [CORES * step for step in range(2, chips)]
    fills = [-count % 8] + [-(CORES * count) % 8] * len(far) + [-count % 8]
    first = (count - sum(fills[:2])) // 8 * 8
    if CORES * count - first - sum(fills) < 8:
        fills = [0] * len(fills)
    begins = [first + sum(fills[:i]) for i in range(len(fills) + 1)]
    last = len(fills) + 1

    own = prepare(tokens, route_ids, route_scores)
    near_same = swap_expert(own, near)
    came = [swap_expert(own, mask) for mask in far]
    theirs, received, kept, hidden, arrived, begun, outs, chunks = {}, {}, {}, {}, {}, {}, {}, {}
    parts, back, after = {}, [], []

    def local(begin, end):
        if end <= count:
            return [own[begin:end]]
        if begin >= count:
            return [partner[begin - count : end - count]]
        return [own[begin:], partner[: end - count]]

    def bring(i, rows):
        chunks[i] = jnp.concatenate(rows + local(begins[i - 1], begins[i]), axis=0)

    def bring_far(i):
        rows = later(came[i - 2], after[0])
        bring(i, [rows, swap_expert(rows, 1)])

    def send_theirs(i, **load):
        theirs[i] = gate_up(chunks[i], gate_other, up_other, bf16, after, **load)
        more = []
        if load:
            theirs[i], *more = theirs[i]
        received[i] = swap_tensor(theirs[i])
        after[:] = [theirs[i]]
        return more

    def keep(i, **load):
        kept[i] = gate_up(chunks[i], gate_mine, up_mine, f32, after, **load)
        more = []
        if load:
            kept[i], *more = kept[i]
        after[:] = [kept[i]]
        return more

    def send_hidden(i):
        hidden[i] = hidden_of(here, chunks[i], kept[i], received[i], local_experts, after)
        arrived[i] = swap_tensor(hidden[i])
        after[:] = [hidden[i]]

    def begin_down(i):
        begun[i] = down(hidden[i], down_mine, None, after, 3 if i == last - 1 else 1)
        after[:] = [begun[i]]

    def end_down(i):
        out = outs[i] = down(arrived[i], down_other, begun[i], after)
        after[:] = [out]
        if i in (1, last - 1):
            back.append(swap_expert(out[:count].astype(bf16), near + (i != 1)))
        elif 1 < i < last:
            from_core = swap_expert(out[count : CORES * count].astype(bf16), 1)
            parts[i] = (out[:count] + from_core.astype(f32)).astype(bf16)
            back.append(swap_expert(parts[i], far[i - 2]))

    chunks[0] = own[:first]
    theirs[0], gate_other, up_other = gate_up_load(other, chunks[0], w_gate, w_up, [here, mine], bf16)
    received[0] = swap_tensor(theirs[0])
    after[:] = [theirs[0]]
    bring(1, [near_same])
    send_theirs(1)
    kept[0], gate_mine, up_mine = gate_up_load(mine, chunks[0], w_gate, w_up, after, f32)
    after[:] = [kept[0]]
    partner = swap_expert(later(own, kept[0]), 1)
    send_hidden(0)
    if far:
        bring_far(2)
    keep(1)
    send_hidden(1)
    near_other = swap_expert(later(own, hidden[1]), near + 1)
    if not far:
        bring(2, [near_other])
    (down_mine,) = send_theirs(2, side=mine, w_down=w_down)
    if len(far) > 1:
        bring_far(3)
    elif far:
        bring(3, [near_other])
    else:
        chunks[3] = partner[begins[-1] - count :]
    (down_other,) = keep(2, side=other, w_down=w_down)
    begin_down(0)
    send_theirs(3)
    begin_down(1)
    for i in range(2, last + 1):
        send_hidden(i)
        if i + 2 <= last:
            if i + 2 == last:
                chunks[last] = partner[begins[-1] - count :]
            elif i + 2 == last - 1:
                bring(i + 2, [later(near_other, hidden[i])])
            else:
                bring_far(i + 2)
            send_theirs(i + 2)
        if i == last - 1:
            keep(last)
        for early in (0, 1) if i == 2 else (i - 1,):
            end_down(early)
        begin_down(i)
        if i + 1 < last:
            keep(i + 1)
        if i - 1 in parts:
            after.append(parts[i - 1])
    end_down(last)

    pieces = [outs[0]]
    for i in range(1, last):
        pieces.append(outs[i][count if i in (1, last - 1) else CORES * count :])
    pieces = jnp.concatenate(pieces + [outs[last]], axis=0)
    from_core = swap_expert(pieces[count:].astype(bf16), 1)
    result = pieces[:count]
    for value in back + [from_core]:
        result = result + value.astype(f32)
    return result.astype(bf16)


def solution(mesh):
    groups = mesh.shape["expert"]
    paired = mesh.shape["tensor"] == 2 and groups > CORES and groups & (groups - 1) == 0
    placed = (
        P(("replica", "expert"), "tensor"),
        P(("replica", "expert"), None),
        P(("replica", "expert"), None),
        P("expert", "tensor", None),
        P("expert", "tensor", None),
        P("expert", None, "tensor"),
    )
    return jax.shard_map(
        pair_shards if paired else general_shards,
        mesh=mesh,
        in_specs=placed,
        out_specs=P(("replica", "expert"), "tensor"),
        check_vma=False,
    )
```
